512 devices in a mesh: dp: 8 (over y, core), head: 64 (over x, z).
Axes of the slice: x: 4, y: 4, z: 16, core: 2. Of those that a mesh axis runs over, the one named last changes fastest.
Arguments:
- head_ids: int32 [8, 8192, 8], P('dp', 'head'), may hold values from 0 to 63, as said below
- query_slots: bfloat16 [8, 8192, 8, 128], P('dp', 'head'), may hold values from -300 to 300
- key_slots: bfloat16 [8, 8192, 8, 128], P('dp', 'head'), may hold values from -13 to 13
- value_slots: bfloat16 [8, 8192, 8, 128], P('dp', 'head'), may hold values from -5 to 5
- gate_logits: float32 [8, 8192, 8], P('dp', 'head'), may hold values from -8 to 310
- sink_logits: float32 [64], P('head'), may hold values from 1 to 6
- out_grad: bfloat16 [8, 8192, 8, 128], P('dp', 'head'), may hold values from -6 to 6
Outputs:
- mixed: bfloat16 [8, 8192, 8, 128], P('dp', 'head')
- query_grad: bfloat16 [8, 8192, 8, 128], P('dp', 'head')
- key_grad: bfloat16 [8, 8192, 8, 128], P('dp', 'head')
- value_grad: bfloat16 [8, 8192, 8, 128], P('dp', 'head')
- gate_grad: float32 [8, 8192, 8], P('dp', 'head')
- sink_grad: float32 [64], P('head')
The draws below stay inside these ranges and needn't reach their ends.
Inputs may be any that keep to these rules, and one draw needn't show every extreme that they name: `head_ids`: each token names 8 different heads. Among the 128 tokens of one device no head is named more than 32 times, and in every group one head is named exactly 32 times by the tokens of every device of that group.
All inputs are finite; a program needn't handle non-finite values.
Results may differ from the reference program's by a relative error of at most 0.023.
Values may be sent and summed in bfloat16 or wider, within the bound.
A program may use at most 64 MiB of HBM per device.

```python
import math
import jax
import jax.numpy as jnp
from jax import lax

HEADS = 64
HDIM = 128
TOPK = 8
TOK_DEV = 128
GROUPS = 8
SEQ = 8192
SLOT = 32
CAP = 2048


def route_block(block_key, hot_head):
    key_order, key_spread, key_others, key_roll = jax.random.split(block_key, 4)
    token_order = jax.random.permutation(key_order, TOK_DEV).astype(jnp.int32)
    rank_of = jnp.zeros((TOK_DEV,), jnp.int32).at[token_order].set(jnp.arange(TOK_DEV, dtype=jnp.int32))
    has_hot = (rank_of < SLOT).astype(jnp.int32)
    needed = TOPK - has_hot
    begin_at = jnp.cumsum(needed) - needed
    spread = jax.random.randint(key_spread, (), HEADS // 2, HEADS)
    others = jax.random.permutation(key_others, HEADS - 1).astype(jnp.int32)
    others = others + (others >= hot_head).astype(jnp.int32)
    column = jnp.arange(TOPK, dtype=jnp.int32)
    pick_index = jnp.mod(begin_at[:, None] + column[None, :] - has_hot[:, None], spread)
    picked = others[pick_index]
    chosen = jnp.where((has_hot[:, None] == 1) & (column[None, :] == 0), hot_head, picked)
    shift_by = jax.random.randint(key_roll, (TOK_DEV, 1), 0, TOPK)
    rolled = jnp.mod(column[None, :] + shift_by, TOPK)
    return jnp.take_along_axis(chosen, rolled, axis=1).astype(jnp.int32)


def route_group(group_key):
    key_hot, key_blocks = jax.random.split(group_key)
    hot_head = jax.random.randint(key_hot, (), 0, HEADS)
    block_keys = jax.random.split(key_blocks, SEQ // TOK_DEV)
    blocks_all = jax.vmap(route_block, in_axes=(0, None))(block_keys, hot_head)
    return blocks_all.reshape(SEQ, TOPK)


def route_ids(key):
    base_key = jax.random.fold_in(key, 11)
    return jax.vmap(route_group)(jax.random.split(base_key, GROUPS))


def draw_head_ids(key, part):
    return route_ids(key)


def slot_vectors(key):
    base_key = jax.random.fold_in(key, 23)
    key_key, key_query = jax.random.split(base_key, 2)
    dims_all = (GROUPS, SEQ, TOPK, HDIM)
    key_base = jnp.clip(jax.random.normal(key_key, dims_all, jnp.float32), -4.0, 4.0)
    queries = jnp.clip(1.5 * jax.random.normal(key_query, dims_all, jnp.float32), -9.0, 9.0)
    return (queries, key_base)


def draw_query_slots(key, part):
    return slot_vectors(key)[0].astype(jnp.bfloat16)


def draw_key_slots(key, part):
    return slot_vectors(key)[1].astype(jnp.bfloat16)


def draw_gate_logits(key, part):
    key_base = jax.random.fold_in(jax.random.fold_in(key, 31), 0)
    dims_all = (GROUPS, SEQ, TOPK)
    return jnp.clip(1.5 * jax.random.normal(key_base, dims_all, jnp.float32), -8.0, 8.0)


def level_of(stream_key, extent, cuts, low, top_value):
    factor_of = 1.0
    for dim, blocks in cuts:
        draws = jax.random.uniform(jax.random.fold_in(jax.random.fold_in(stream_key, 6), dim), (blocks,), jnp.float32, low / len(cuts), top_value / len(cuts))
        factor_of = factor_of * jnp.repeat(jnp.exp(draws), extent[dim] // blocks).reshape((-1,) + (1,) * (len(extent) - 1 - dim))
    return factor_of


def bell_draw(rng, extent, scale, reach, cuts=(), kind=jnp.bfloat16):
    gain = level_of(rng, extent, cuts, -0.22, 0.18) if cuts else 1.0
    drawn = jax.random.normal(rng, extent, jnp.float32) * scale * gain
    return jnp.minimum(jnp.maximum(drawn, -reach), reach).astype(kind)


def setup_inputs(seed: int = 0) -> dict:
    key_list = jax.random.split(jax.random.key(seed), 8)
    return {
        "head_ids": draw_head_ids(jax.random.fold_in(key_list[7], 71), 0),
        "query_slots": draw_query_slots(jax.random.fold_in(key_list[7], 71), 0),
        "key_slots": draw_key_slots(jax.random.fold_in(key_list[7], 71), 0),
        "value_slots": bell_draw(key_list[3], (GROUPS, SEQ, TOPK, HDIM), 1.0, 5.0, ((0, 8), (1, 64))),
        "gate_logits": draw_gate_logits(jax.random.fold_in(key_list[7], 71), 0),
        "sink_logits": jnp.clip(1.0 + 5.0 * jax.random.uniform(key_list[5], (HEADS,), jnp.float32) ** level_of(key_list[5], (HEADS,), ((0, 64),), -0.2, 0.2), 1.0, 6.0),
        "out_grad": bell_draw(key_list[6], (GROUPS, SEQ, TOPK, HDIM), 1.0, 6.0, ((0, 8), (1, 64))),
    }


masked_value = -1e+30

def head_terms(head_flat, query_flat, key_flat, value_flat, cot_flat, sink_value, head):
    index_list = jnp.argsort((head_flat != head).astype(jnp.int32), stable=True)[:CAP].astype(jnp.int32)
    live_rows = head_flat[index_list] == head
    position = index_list // TOPK
    query_rows = query_flat[index_list]
    key_rows = key_flat[index_list]
    value_rows = value_flat[index_list]
    cot_rows = jnp.where(live_rows[:, None], cot_flat[index_list], jnp.zeros((), jnp.bfloat16))
    scale = 1.0 / math.sqrt(HDIM)
    scores = scale * jnp.dot(query_rows, key_rows.T, preferred_element_type=jnp.float32)
    allowed = live_rows[:, None] & live_rows[None, :] & (position[None, :] <= position[:, None])
    masked = jnp.where(allowed, scores, masked_value)
    row_max = jnp.maximum(lax.optimization_barrier(jnp.max(masked, axis=1)), sink_value)
    row_sum = jnp.exp(sink_value - row_max) + lax.optimization_barrier(jnp.sum(jnp.where(allowed, jnp.exp(masked - row_max[:, None]), 0.0), axis=1))
    row_lse = row_max + jnp.log(row_sum)
    probability = jnp.where(allowed, jnp.exp(scores - row_lse[:, None]), 0.0)
    weights = probability.astype(jnp.bfloat16)
    head_out = jnp.dot(weights, value_rows, preferred_element_type=jnp.float32).astype(jnp.bfloat16)
    deltas = lax.optimization_barrier(jnp.sum(cot_rows.astype(jnp.float32) * head_out.astype(jnp.float32), axis=1))
    dprob = jnp.dot(cot_rows, value_rows.T, preferred_element_type=jnp.float32)
    dscore = (probability * (dprob - deltas[:, None])).astype(jnp.bfloat16)
    query_grad = (scale * jnp.dot(dscore, key_rows, preferred_element_type=jnp.float32)).astype(jnp.bfloat16)
    key_grad = (scale * jnp.dot(dscore.T, query_rows, preferred_element_type=jnp.float32)).astype(jnp.bfloat16)
    value_grad = jnp.dot(weights.T, cot_rows, preferred_element_type=jnp.float32).astype(jnp.bfloat16)
    sink_grad = -jnp.sum(jnp.exp(sink_value - row_lse) * deltas)
    return (index_list, live_rows, head_out, query_grad, key_grad, value_grad, sink_grad)

def group_terms(head_flat, query_flat, key_flat, value_flat, cot_flat, sink_logits):

    def per_head(carry, head):
        out_acc, qgrad_acc, kgrad_acc, vgrad_acc = carry
        index_list, live_rows, head_out, query_grad, key_grad, value_grad, sink_grad = head_terms(head_flat, query_flat, key_flat, value_flat, cot_flat, sink_logits[head], head)

        def add_to(total, values):
            return total.at[index_list].add(jnp.where(live_rows[:, None], values.astype(jnp.float32), jnp.zeros((), jnp.float32)))
        return ((add_to(out_acc, head_out), add_to(qgrad_acc, query_grad), add_to(kgrad_acc, key_grad), add_to(vgrad_acc, value_grad)), sink_grad)
    zeros_all = jnp.zeros((SEQ * TOPK, HDIM), jnp.float32)
    totals, sink_grads = lax.scan(per_head, (zeros_all, zeros_all, zeros_all, zeros_all), jnp.arange(HEADS, dtype=jnp.int32))
    return tuple((item.astype(jnp.bfloat16) for item in totals)) + (sink_grads,)

def reference(head_ids, query_slots, key_slots, value_slots, gate_logits, sink_logits, out_grad):
    gate_probs = jax.nn.softmax(gate_logits, axis=-1)
    cotangent = (gate_probs[..., None] * out_grad.astype(jnp.float32)).astype(jnp.bfloat16)

    def one_group(group):
        return group_terms(head_ids[group].reshape(-1), query_slots[group].reshape(-1, HDIM), key_slots[group].reshape(-1, HDIM), value_slots[group].reshape(-1, HDIM), cotangent[group].reshape(-1, HDIM), sink_logits)
    head_out, query_grad, key_grad, value_grad, sink_grads = lax.map(one_group, jnp.arange(GROUPS, dtype=jnp.int32))
    full_shape = (GROUPS, SEQ, TOPK, HDIM)
    head_out = head_out.reshape(full_shape)
    mixed = (gate_probs[..., None] * head_out.astype(jnp.float32)).astype(jnp.bfloat16)
    gate_sum = lax.optimization_barrier(jnp.sum(out_grad.astype(jnp.float32) * head_out.astype(jnp.float32), axis=-1))
    gate_grad = gate_probs * (gate_sum - lax.optimization_barrier(jnp.sum(gate_probs * gate_sum, axis=-1, keepdims=True)))
    sink_grad = lax.optimization_barrier(jnp.sum(sink_grads, axis=0))
    return (mixed, query_grad.reshape(full_shape), key_grad.reshape(full_shape), value_grad.reshape(full_shape), gate_grad, sink_grad)
```

```python
import math

import jax
import jax.numpy as jnp
from jax import lax
from jax.experimental import pallas as pl
from jax.experimental.pallas import tpu as pltpu
from jax.sharding import PartitionSpec as P

HEADS = 64
SLOT = 32
DEAD = 2.0**100
MASKED = -1e30
BLOCK = 256
MESH = pl.DeviceIdType.MESH
f32, bf16 = jnp.float32, jnp.bfloat16


def dot(a, b, dims=((1,), (0,))):
    return lax.dot_general(a, b, (dims, ((), ())), preferred_element_type=f32)


def iota(shape, dim):
    return lax.broadcasted_iota(jnp.int32, shape, dim)


def one_hot(mask):
    return jnp.where(mask, 1.0, 0.0).astype(bf16)


def block_at(n):
    return pl.ds(pl.multiple_of(n * BLOCK, BLOCK), BLOCK)


def places(ids, rows):
    slots, tokens = ids.shape
    head = iota((HEADS, tokens), 0)
    named = [head == ids[j : j + 1] for j in range(slots)]
    count = sum(jnp.where(mask, 1.0, 0.0) for mask in named).astype(bf16)
    earlier = dot(count, one_hot(iota((tokens, tokens), 0) < iota((tokens, tokens), 1)))
    rank = jnp.concatenate(
        [jnp.sum(jnp.where(mask, earlier, 0.0), axis=0, keepdims=True) for mask in named], axis=0
    )
    spread = one_hot(iota((tokens, rows), 0) == iota((tokens, rows), 1) // slots)
    place = dot(ids.astype(f32).astype(bf16), spread) * SLOT + dot(rank.astype(bf16), spread)
    mine = iota((slots, rows), 0) == iota((slots, rows), 1) % slots
    return jnp.sum(jnp.where(mine, place, 0.0), axis=0, keepdims=True).astype(jnp.int32)


def pack(place, wide, send):
    rows, width = wide.shape[0], wide.shape[1] // 4
    ones = jnp.ones((rows, width), bf16)

    def chunk(c, carry):
        slot = c * BLOCK + iota((BLOCK, rows), 0)
        pick = one_hot(slot == place)
        moved = dot(pick, wide[...])
        live = dot(pick, ones)
        for a in range(4):
            part = moved[:, a * width : (a + 1) * width]
            if a == 1:
                part = jnp.where((live < 0.5) & (iota((BLOCK, width), 1) == 0), DEAD, part)
            send[a, block_at(c), :] = part.astype(bf16)
        return carry

    lax.fori_loop(0, send.shape[1] // BLOCK, chunk, 0)


def forward(recv, sink, out, probs, strip, bias, sink_share, factor):
    blocks = recv.shape[1] // BLOCK
    half = recv.shape[2]
    first = one_hot(iota((8, half), 1) == 0)

    def bias_block(j, carry):
        mark = dot(first, recv[1, block_at(j), :], ((1,), (1,)))
        bias[j] = jnp.where(mark > 0.5 * DEAD, MASKED, 0.0)
        return carry

    lax.fori_loop(0, blocks, bias_block, 0)
    causal = iota((BLOCK, BLOCK), 1) <= iota((BLOCK, BLOCK), 0)

    def query_block(i, carry):
        query = recv[0, block_at(i), :]

        def scores(j):
            raw = dot(query, recv[1, block_at(j), :], ((1,), (1,))) * factor
            return jnp.where(bias[j][0:1] < 0.0, MASKED, raw)

        def halves(tile):
            return [tile[:, n * half : (n + 1) * half] for n in range(BLOCK // half)]

        def score_step(j, top):
            tile = scores(j)
            strip[j] = tile
            for part in halves(tile):
                top = jnp.maximum(top, part)
            return top

        top = lax.fori_loop(0, i, score_step, jnp.full((BLOCK, half), sink, f32))
        tile = jnp.where(causal, scores(i), MASKED)
        strip[i] = tile
        for part in halves(tile):
            top = jnp.maximum(top, part)
        top = jnp.max(top, axis=1, keepdims=True)

        def sum_step(j, total):
            weight = jnp.exp2(strip[j] - top)
            strip[j] = weight
            for part in halves(weight):
                total = total + part
            return total

        zero = jnp.zeros((BLOCK, half), f32)
        total = lax.fori_loop(0, i + 1, sum_step, zero)
        sink_part = jnp.exp2(sink - top)
        scale = 1.0 / (jnp.sum(total, axis=1, keepdims=True) + sink_part)

        def value_step(j, acc):
            weight = (strip[j] * scale).astype(bf16)
            probs[i, j] = weight
            return acc + dot(weight, recv[2, block_at(j), :])

        acc = lax.fori_loop(0, i + 1, value_step, zero)
        out[0, block_at(i), :] = acc.astype(bf16)
        sink_share[block_at(i), :] = jnp.broadcast_to(sink_part * scale, (BLOCK, half))
        return carry

    lax.fori_loop(0, blocks, query_block, 0)


def backward(recv, out, probs, sink_share, kgrad, vgrad, root):
    blocks = recv.shape[1] // BLOCK
    width = recv.shape[2]
    kgrad[...] = jnp.zeros_like(kgrad)
    vgrad[...] = jnp.zeros_like(vgrad)

    def query_block(i, sink_sum):
        at = block_at(i)
        query, cot = recv[0, at, :], recv[3, at, :]
        delta = jnp.sum(cot.astype(f32) * out[0, at, :].astype(f32), axis=1, keepdims=True)
        sink_sum = sink_sum - jnp.sum(sink_share[at, :] * delta, axis=0, keepdims=True)

        def key_step(j, qgrad):
            there = block_at(j)
            keys, values = recv[1, there, :], recv[2, there, :]
            weight = probs[i, j]
            dprob = dot(cot, values, ((1,), (1,)))
            dscore = (weight.astype(f32) * (dprob - delta)).astype(bf16)
            kgrad[there, :] += dot(dscore, query, ((0,), (0,)))
            vgrad[there, :] += dot(weight, cot, ((0,), (0,)))
            return qgrad + dot(dscore, keys)

        qgrad = lax.fori_loop(0, i + 1, key_step, jnp.zeros((BLOCK, width), f32))
        out[1, at, :] = (root * qgrad).astype(bf16)
        return sink_sum

    sink_sum = lax.fori_loop(0, blocks, query_block, jnp.zeros((1, width), f32))

    def round_block(j, carry):
        there = block_at(j)
        out[2, there, :] = (root * kgrad[there, :]).astype(bf16)
        out[3, there, :] = vgrad[there, :].astype(bf16)
        return carry

    lax.fori_loop(0, blocks, round_block, 0)
    return sink_sum


def whole_kernel(
    groups,
    devices,
    ids_ref,
    gate_ref,
    sink_ref,
    q_ref,
    k_ref,
    v_ref,
    og_ref,
    mixed_ref,
    qg_ref,
    kg_ref,
    vg_ref,
    gg_ref,
    sink_out,
    wide,
    og,
    gate_rows,
    gate_sums,
    place_col,
    pick,
    send,
    recv,
    ret,
    back,
    probs,
    strip,
    bias,
    sink_share,
    kgrad,
    vgrad,
    sink_mine,
    sink_all,
    load,
    near,
    sent,
    got,
):
    dp, me = lax.axis_index("dp"), lax.axis_index("head")
    rows, width = q_ref.shape
    tokens, slots, _ = og.shape

    def peers(body):
        def step(n, carry):
            body(lax.rem(me + n, devices))
            return carry

        lax.fori_loop(1, devices, step, 0)

    def group_peers(body):
        def step(n, carry):
            body(lax.rem(dp + n, groups))
            return carry

        lax.fori_loop(1, groups, step, 0)

    loads = [
        pltpu.make_async_copy(ref, wide.at[:, pl.ds(a * width, width)], load.at[a])
        for a, ref in enumerate((q_ref, k_ref, v_ref))
    ] + [pltpu.make_async_copy(og_ref, og, load.at[3])]
    for copy in loads:
        copy.start()
    barrier = pltpu.get_barrier_semaphore()
    peers(lambda d: pl.semaphore_signal(barrier, 1, device_id=(dp, d), device_id_type=MESH))
    group_peers(lambda g: pl.semaphore_signal(barrier, 1, device_id=(g, me), device_id_type=MESH))

    logits = gate_ref[...]
    shifted = jnp.exp(logits - jnp.max(logits, axis=0, keepdims=True))
    gate_rows[...] = (shifted / jnp.sum(shifted, axis=0, keepdims=True)).T
    place = places(ids_ref[...], rows)
    for copy in loads:
        copy.wait()
    cot = gate_rows[...][:, :, None] * og[...].astype(f32)
    wide[:, 3 * width :] = cot.astype(bf16).reshape(rows, width)
    pack(place, wide, send)
    pl.semaphore_wait(barrier, devices - 1 + groups - 1)

    def at(d):
        return pl.ds(pl.multiple_of(d * SLOT, SLOT), SLOT)

    stages = (
        (send, recv, pl.ds(0, 3)),
        (send, recv, pl.ds(3, 1)),
        (ret, back, pl.ds(0, 1)),
        (ret, back, pl.ds(1, 1)),
        (ret, back, pl.ds(2, 1)),
        (ret, back, pl.ds(3, 1)),
    )

    def own(phase):
        source, target, arrays = stages[phase]
        return pltpu.make_async_copy(
            source.at[arrays, at(me)], target.at[arrays, at(me)], near.at[phase]
        )

    def begin(phase):
        source, target, arrays = stages[phase]
        own(phase).start()
        peers(
            lambda d: pltpu.make_async_remote_copy(
                src_ref=source.at[arrays, at(d)],
                dst_ref=target.at[arrays, at(me)],
                send_sem=sent.at[phase],
                recv_sem=got.at[phase],
                device_id=(dp, d),
                device_id_type=MESH,
            ).start()
        )

    def all_of(ref, arrays, sem):
        piece = ref.at[arrays, pl.ds(0, (devices - 1) * SLOT)]
        pltpu.make_async_copy(piece, piece, sem).wait()

    def arrived(phase):
        _, target, arrays = stages[phase]
        own(phase).wait()
        all_of(target, arrays, got.at[phase])

    root = 1.0 / math.sqrt(width)
    begin(0)
    begin(1)
    place_col[...] = jnp.broadcast_to(place, (8, rows)).T

    def pick_block(c, carry):
        slot = iota((BLOCK, HEADS * SLOT), 1)
        pick[block_at(c), :] = one_hot(slot == place_col[block_at(c), 0:1])
        return carry

    lax.fori_loop(0, rows // BLOCK, pick_block, 0)
    arrived(0)
    sink = sink_ref[0] * math.log2(math.e)
    forward(recv, sink, ret, probs, strip, bias, sink_share, root * math.log2(math.e))
    begin(2)
    arrived(1)
    sink_sum = backward(recv, ret, probs, sink_share, kgrad, vgrad, root)
    for phase in (3, 4, 5):
        begin(phase)
    sink_mine[...] = jnp.broadcast_to(sink_sum, sink_mine.shape)
    group_peers(
        lambda g: pltpu.make_async_remote_copy(
            src_ref=sink_mine,
            dst_ref=sink_all.at[dp],
            send_sem=sent.at[6],
            recv_sem=got.at[6],
            device_id=(g, me),
            device_id_type=MESH,
        ).start()
    )
    own_sink = pltpu.make_async_copy(sink_mine, sink_all.at[dp], near.at[6])
    own_sink.start()

    step = BLOCK // slots

    def collect(a, store):
        def chunk(c, carry):
            part = dot(pick[block_at(c), :], back[a])
            store(pl.ds(pl.multiple_of(c * step, step), step), part.reshape(step, slots, width))
            return carry

        lax.fori_loop(0, rows // BLOCK, chunk, 0)

    def store_mixed(here, part):
        mixed_ref[here] = (gate_rows[here][:, :, None] * part).astype(bf16)
        gate_sums[here] = jnp.sum(og[here].astype(f32) * part, axis=-1)

    arrived(2)
    collect(0, store_mixed)
    gate = gate_rows[...]
    gate_sum = gate_sums[...]
    mean = jnp.sum(gate * gate_sum, axis=-1, keepdims=True)
    gg_ref[...] = (gate * (gate_sum - mean)).T
    others = sink_all.at[pl.ds(0, groups - 1)]
    pltpu.make_async_copy(others, others, got.at[6]).wait()
    own_sink.wait()
    sink_out[0] = jnp.sum(jnp.sum(sink_all[...], axis=0)[0:1, 0:1])
    for a, ref in ((1, qg_ref), (2, kg_ref), (3, vg_ref)):
        arrived(a + 2)

        def store(here, part, ref=ref):
            ref[here] = part.astype(bf16)

        collect(a, store)
    for phase, (source, _, arrays) in enumerate(stages):
        all_of(source, arrays, sent.at[phase])
    pltpu.make_async_copy(others, others, sent.at[6]).wait()


def whole(groups, devices, ids, gate_logits, sink_logits, q, k, v, og):
    tokens, slots, width = og.shape
    rows = tokens * slots
    padded = HEADS * SLOT
    blocks = padded // BLOCK
    vmem = pl.BlockSpec(memory_space=pltpu.VMEM)
    smem = pl.BlockSpec(memory_space=pltpu.SMEM)
    hbm = pl.BlockSpec(memory_space=pl.ANY)
    grad = jax.ShapeDtypeStruct((tokens, slots, width), bf16)

    def body(*refs):
        whole_kernel(groups, devices, *refs)

    return pl.pallas_call(
        body,
        out_shape=(grad,) * 4
        + (jax.ShapeDtypeStruct((slots, tokens), f32), jax.ShapeDtypeStruct((1,), f32)),
        in_specs=[vmem, vmem, smem, hbm, hbm, hbm, hbm],
        out_specs=(vmem,) * 5 + (smem,),
        scratch_shapes=[
            pltpu.VMEM((rows, 4 * width), bf16),
            pltpu.VMEM((tokens, slots, width), bf16),
            pltpu.VMEM((tokens, slots), f32),
            pltpu.VMEM((tokens, slots), f32),
            pltpu.VMEM((rows, 8), jnp.int32),
            pltpu.VMEM((rows, padded), bf16),
            pltpu.VMEM((4, padded, width), bf16),
            pltpu.VMEM((4, padded, width), bf16),
            pltpu.VMEM((4, padded, width), bf16),
            pltpu.VMEM((4, padded, width), bf16),
            pltpu.VMEM((blocks, blocks, BLOCK, BLOCK), bf16),
            pltpu.VMEM((blocks, BLOCK, BLOCK), f32),
            pltpu.VMEM((blocks, 8, BLOCK), f32),
            pltpu.VMEM((padded, width), f32),
            pltpu.VMEM((padded, width), f32),
            pltpu.VMEM((padded, width), f32),
            pltpu.VMEM((8, width), f32),
            pltpu.VMEM((groups, 8, width), f32),
            pltpu.SemaphoreType.DMA((4,)),
            pltpu.SemaphoreType.DMA((7,)),
            pltpu.SemaphoreType.DMA((7,)),
            pltpu.SemaphoreType.DMA((7,)),
        ],
        compiler_params=pltpu.CompilerParams(
            collective_id=0, has_side_effects=True, vmem_limit_bytes=60 * 2**20
        ),
    )(
        ids,
        gate_logits,
        sink_logits,
        q.reshape(rows, width),
        k.reshape(rows, width),
        v.reshape(rows, width),
        og,
    )


def per_device(head_ids, query_slots, key_slots, value_slots, gate_logits, sink_logits, out_grad):
    mixed, qgrad, kgrad, vgrad, gate_grad, sink_grad = whole(
        lax.axis_size("dp"),
        lax.axis_size("head"),
        head_ids[0].T,
        gate_logits[0].T,
        sink_logits,
        query_slots[0],
        key_slots[0],
        value_slots[0],
        out_grad[0],
    )
    return mixed[None], qgrad[None], kgrad[None], vgrad[None], gate_grad.T[None], sink_grad


def solution(mesh):
    rows3 = P("dp", "head", None)
    rows4 = P("dp", "head", None, None)
    return jax.shard_map(
        per_device,
        mesh=mesh,
        in_specs=(rows3, rows4, rows4, rows4, rows3, P("head"), rows4),
        out_specs=(rows4, rows4, rows4, rows4, rows3, P("head")),
        check_vma=False,
    )
```

```python
import math

import jax
import jax.numpy as jnp
from jax import lax
from jax.experimental import pallas as pl
from jax.experimental.pallas import tpu as pltpu
from jax.sharding import PartitionSpec as P

HEADS = 64
SLOT = 32
DEAD = 2.0**100
MASKED = -1e30
BLOCK = 256
MESH = pl.DeviceIdType.MESH
f32, bf16 = jnp.float32, jnp.bfloat16


def dot(a, b, dims=((1,), (0,))):
    return lax.dot_general(a, b, (dims, ((), ())), preferred_element_type=f32)


def iota(shape, dim):
    return lax.broadcasted_iota(jnp.int32, shape, dim)


def one_hot(mask):
    return jnp.where(mask, 1.0, 0.0).astype(bf16)


def block_at(n):
    return pl.ds(pl.multiple_of(n * BLOCK, BLOCK), BLOCK)


def places(ids, rows):
    slots, tokens = ids.shape
    head = iota((HEADS, tokens), 0)
    named = [head == ids[j : j + 1] for j in range(slots)]
    count = sum(jnp.where(mask, 1.0, 0.0) for mask in named).astype(bf16)
    earlier = dot(count, one_hot(iota((tokens, tokens), 0) < iota((tokens, tokens), 1)))
    rank = jnp.concatenate(
        [jnp.sum(jnp.where(mask, earlier, 0.0), axis=0, keepdims=True) for mask in named], axis=0
    )
    spread = one_hot(iota((tokens, rows), 0) == iota((tokens, rows), 1) // slots)
    place = dot(ids.astype(f32).astype(bf16), spread) * SLOT + dot(rank.astype(bf16), spread)
    mine = iota((slots, rows), 0) == iota((slots, rows), 1) % slots
    return jnp.sum(jnp.where(mine, place, 0.0), axis=0, keepdims=True).astype(jnp.int32)


def pack(place, wide, send):
    rows, width = wide.shape[0], wide.shape[1] // 4
    ones = jnp.ones((rows, width), bf16)

    def chunk(c, carry):
        slot = c * BLOCK + iota((BLOCK, rows), 0)
        pick = one_hot(slot == place)
        moved = dot(pick, wide[...])
        live = dot(pick, ones)
        for a in range(4):
            part = moved[:, a * width : (a + 1) * width]
            if a == 1:
                part = jnp.where((live < 0.5) & (iota((BLOCK, width), 1) == 0), DEAD, part)
            send[a, block_at(c), :] = part.astype(bf16)
        return carry

    lax.fori_loop(0, send.shape[1] // BLOCK, chunk, 0)


def forward(recv, sink, out, probs, strip, bias, sink_share, factor):
    blocks = recv.shape[1] // BLOCK
    half = recv.shape[2]
    first = one_hot(iota((8, half), 1) == 0)

    def bias_block(j, carry):
        mark = dot(first, recv[1, block_at(j), :], ((1,), (1,)))
        bias[j] = jnp.where(mark > 0.5 * DEAD, MASKED, 0.0)
        return carry

    lax.fori_loop(0, blocks, bias_block, 0)
    causal = iota((BLOCK, BLOCK), 1) <= iota((BLOCK, BLOCK), 0)

    def query_block(i, carry):
        query = recv[0, block_at(i), :]

        def scores(j):
            raw = dot(query, recv[1, block_at(j), :], ((1,), (1,))) * factor
            return jnp.where(bias[j][0:1] < 0.0, MASKED, raw)

        def halves(tile):
            return [tile[:, n * half : (n + 1) * half] for n in range(BLOCK // half)]

        def score_step(j, top):
            tile = scores(j)
            strip[j] = tile
            for part in halves(tile):
                top = jnp.maximum(top, part)
            return top

        top = lax.fori_loop(0, i, score_step, jnp.full((BLOCK, half), sink, f32))
        tile = jnp.where(causal, scores(i), MASKED)
        strip[i] = tile
        for part in halves(tile):
            top = jnp.maximum(top, part)
        top = jnp.max(top, axis=1, keepdims=True)

        def sum_step(j, total):
            weight = jnp.exp2(strip[j] - top)
            strip[j] = weight
            for part in halves(weight):
                total = total + part
            return total

        zero = jnp.zeros((BLOCK, half), f32)
        total = lax.fori_loop(0, i + 1, sum_step, zero)
        sink_part = jnp.exp2(sink - top)
        scale = 1.0 / (jnp.sum(total, axis=1, keepdims=True) + sink_part)

        def value_step(j, acc):
            weight = (strip[j] * scale).astype(bf16)
            probs[i, j] = weight
            return acc + dot(weight, recv[2, block_at(j), :])

        acc = lax.fori_loop(0, i + 1, value_step, zero)
        out[0, block_at(i), :] = acc.astype(bf16)
        sink_share[block_at(i), :] = jnp.broadcast_to(sink_part * scale, (BLOCK, half))
        return carry

    lax.fori_loop(0, blocks, query_block, 0)


def backward(recv, out, probs, sink_share, kgrad, vgrad, root):
    blocks = recv.shape[1] // BLOCK
    width = recv.shape[2]
    kgrad[...] = jnp.zeros_like(kgrad)
    vgrad[...] = jnp.zeros_like(vgrad)

    def query_block(i, sink_sum):
        at = block_at(i)
        query, cot = recv[0, at, :], recv[3, at, :]
        delta = jnp.sum(cot.astype(f32) * out[0, at, :].astype(f32), axis=1, keepdims=True)
        sink_sum = sink_sum - jnp.sum(sink_share[at, :] * delta, axis=0, keepdims=True)

        def key_step(j, qgrad):
            there = block_at(j)
            keys, values = recv[1, there, :], recv[2, there, :]
            weight = probs[i, j]
            dprob = dot(cot, values, ((1,), (1,)))
            dscore = (weight.astype(f32) * (dprob - delta)).astype(bf16)
            kgrad[there, :] += dot(dscore, query, ((0,), (0,)))
            vgrad[there, :] += dot(weight, cot, ((0,), (0,)))
            return qgrad + dot(dscore, keys)

        qgrad = lax.fori_loop(0, i + 1, key_step, jnp.zeros((BLOCK, width), f32))
        out[1, at, :] = (root * qgrad).astype(bf16)
        return sink_sum

    sink_sum = lax.fori_loop(0, blocks, query_block, jnp.zeros((1, width), f32))

    def round_block(j, carry):
        there = block_at(j)
        out[2, there, :] = (root * kgrad[there, :]).astype(bf16)
        out[3, there, :] = vgrad[there, :].astype(bf16)
        return carry

    lax.fori_loop(0, blocks, round_block, 0)
    return sink_sum


def whole_kernel(
    groups,
    devices,
    ids_hbm,
    gate_hbm,
    sink_ref,
    q_ref,
    k_ref,
    v_ref,
    og_ref,
    mixed_ref,
    qg_ref,
    kg_ref,
    vg_ref,
    gg_ref,
    sink_out,
    ids_ref,
    gate_ref,
    wide,
    og,
    gate_rows,
    gate_sums,
    place_col,
    pick,
    send,
    recv,
    ret,
    back,
    probs,
    strip,
    bias,
    sink_share,
    kgrad,
    vgrad,
    sink_mine,
    sink_all,
    load,
    near,
    sent,
    got,
):
    dp, me = lax.axis_index("dp"), lax.axis_index("head")
    rows, width = q_ref.shape
    tokens, slots, _ = og.shape

    def peers(body):
        def step(n, carry):
            body(lax.rem(me + n, devices))
            return carry

        lax.fori_loop(1, devices, step, 0)

    def group_peers(body):
        def step(n, carry):
            body(lax.rem(dp + n, groups))
            return carry

        lax.fori_loop(1, groups, step, 0)

    loads = [
        pltpu.make_async_copy(ref, wide.at[:, pl.ds(a * width, width)], load.at[a])
        for a, ref in enumerate((q_ref, k_ref, v_ref))
    ] + [
        pltpu.make_async_copy(ref, held, load.at[a])
        for a, ref, held in (
            (3, og_ref, og),
            (4, ids_hbm, ids_ref),
            (5, gate_hbm, gate_ref),
        )
    ]
    for copy in loads:
        copy.start()
    barrier = pltpu.get_barrier_semaphore()
    peers(lambda d: pl.semaphore_signal(barrier, 1, device_id=(dp, d), device_id_type=MESH))
    group_peers(lambda g: pl.semaphore_signal(barrier, 1, device_id=(g, me), device_id_type=MESH))

    for copy in loads:
        copy.wait()
    logits = gate_ref[...]
    shifted = jnp.exp(logits - jnp.max(logits, axis=0, keepdims=True))
    gate_rows[...] = (shifted / jnp.sum(shifted, axis=0, keepdims=True)).T
    place = places(ids_ref[...], rows)
    cot = gate_rows[...][:, :, None] * og[...].astype(f32)
    wide[:, 3 * width :] = cot.astype(bf16).reshape(rows, width)

    pack(place, wide, send)
    pl.semaphore_wait(barrier, devices - 1 + groups - 1)

    def at(d):
        return pl.ds(pl.multiple_of(d * SLOT, SLOT), SLOT)

    stages = (
        (send, recv, pl.ds(0, 3)),
        (send, recv, pl.ds(3, 1)),
        (ret, back, pl.ds(0, 1)),
        (ret, back, pl.ds(1, 1)),
        (ret, back, pl.ds(2, 1)),
        (ret, back, pl.ds(3, 1)),
    )

    def own(phase):
        source, target, arrays = stages[phase]
        return pltpu.make_async_copy(
            source.at[arrays, at(me)], target.at[arrays, at(me)], near.at[phase]
        )

    def begin(phase):
        source, target, arrays = stages[phase]
        own(phase).start()
        peers(
            lambda d: pltpu.make_async_remote_copy(
                src_ref=source.at[arrays, at(d)],
                dst_ref=target.at[arrays, at(me)],
                send_sem=sent.at[phase],
                recv_sem=got.at[phase],
                device_id=(dp, d),
                device_id_type=MESH,
            ).start()
        )

    def all_of(ref, arrays, sem):
        piece = ref.at[arrays, pl.ds(0, (devices - 1) * SLOT)]
        pltpu.make_async_copy(piece, piece, sem).wait()

    def arrived(phase):
        _, target, arrays = stages[phase]
        own(phase).wait()
        all_of(target, arrays, got.at[phase])

    root = 1.0 / math.sqrt(width)
    begin(0)
    begin(1)
    place_col[...] = jnp.broadcast_to(place, (8, rows)).T

    def pick_block(c, carry):
        slot = iota((BLOCK, HEADS * SLOT), 1)
        pick[block_at(c), :] = one_hot(slot == place_col[block_at(c), 0:1])
        return carry

    lax.fori_loop(0, rows // BLOCK, pick_block, 0)
    arrived(0)
    sink = sink_ref[0] * math.log2(math.e)
    forward(recv, sink, ret, probs, strip, bias, sink_share, root * math.log2(math.e))
    begin(2)
    arrived(1)
    sink_sum = backward(recv, ret, probs, sink_share, kgrad, vgrad, root)
    for phase in (3, 4, 5):
        begin(phase)
    sink_mine[...] = jnp.broadcast_to(sink_sum, sink_mine.shape)
    group_peers(
        lambda g: pltpu.make_async_remote_copy(
            src_ref=sink_mine,
            dst_ref=sink_all.at[dp],
            send_sem=sent.at[6],
            recv_sem=got.at[6],
            device_id=(g, me),
            device_id_type=MESH,
        ).start()
    )
    own_sink = pltpu.make_async_copy(sink_mine, sink_all.at[dp], near.at[6])
    own_sink.start()

    step = BLOCK // slots

    def collect(a, store):
        def chunk(c, carry):
            part = dot(pick[block_at(c), :], back[a])
            store(pl.ds(pl.multiple_of(c * step, step), step), part.reshape(step, slots, width))
            return carry

        lax.fori_loop(0, rows // BLOCK, chunk, 0)

    def store_mixed(here, part):
        mixed_ref[here] = (gate_rows[here][:, :, None] * part).astype(bf16)
        gate_sums[here] = jnp.sum(og[here].astype(f32) * part, axis=-1)

    arrived(2)
    collect(0, store_mixed)
    gate = gate_rows[...]
    gate_sum = gate_sums[...]
    mean = jnp.sum(gate * gate_sum, axis=-1, keepdims=True)
    gg_ref[...] = (gate * (gate_sum - mean)).T
    others = sink_all.at[pl.ds(0, groups - 1)]
    pltpu.make_async_copy(others, others, got.at[6]).wait()
    own_sink.wait()
    sink_out[0] = jnp.sum(jnp.sum(sink_all[...], axis=0)[0:1, 0:1])
    for a, ref in ((1, qg_ref), (2, kg_ref), (3, vg_ref)):
        arrived(a + 2)

        def store(here, part, ref=ref):
            ref[here] = part.astype(bf16)

        collect(a, store)
    for phase, (source, _, arrays) in enumerate(stages):
        all_of(source, arrays, sent.at[phase])
    pltpu.make_async_copy(others, others, sent.at[6]).wait()


def held(array):
    return pltpu.with_memory_space_constraint(array, pltpu.HBM)


def whole(groups, devices, ids, gate_logits, sink_logits, q, k, v, og):
    tokens, slots, width = og.shape
    rows = tokens * slots
    padded = HEADS * SLOT
    blocks = padded // BLOCK
    vmem = pl.BlockSpec(memory_space=pltpu.VMEM)
    smem = pl.BlockSpec(memory_space=pltpu.SMEM)
    hbm = pl.BlockSpec(memory_space=pltpu.HBM)
    grad = jax.ShapeDtypeStruct((tokens, slots, width), bf16)

    def body(*refs):
        whole_kernel(groups, devices, *refs)

    return pl.pallas_call(
        body,
        out_shape=(grad,) * 4
        + (jax.ShapeDtypeStruct((slots, tokens), f32), jax.ShapeDtypeStruct((1,), f32)),
        in_specs=[hbm, hbm, smem, hbm, hbm, hbm, hbm],
        out_specs=(vmem,) * 5 + (smem,),
        scratch_shapes=[
            pltpu.VMEM((slots, tokens), jnp.int32),
            pltpu.VMEM((slots, tokens), f32),
            pltpu.VMEM((rows, 4 * width), bf16),
            pltpu.VMEM((tokens, slots, width), bf16),
            pltpu.VMEM((tokens, slots), f32),
            pltpu.VMEM((tokens, slots), f32),
            pltpu.VMEM((rows, 8), jnp.int32),
            pltpu.VMEM((rows, padded), bf16),
            pltpu.VMEM((4, padded, width), bf16),
            pltpu.VMEM((4, padded, width), bf16),
            pltpu.VMEM((4, padded, width), bf16),
            pltpu.VMEM((4, padded, width), bf16),
            pltpu.VMEM((blocks, blocks, BLOCK, BLOCK), bf16),
            pltpu.VMEM((blocks, BLOCK, BLOCK), f32),
            pltpu.VMEM((blocks, 8, BLOCK), f32),
            pltpu.VMEM((padded, width), f32),
            pltpu.VMEM((padded, width), f32),
            pltpu.VMEM((padded, width), f32),
            pltpu.VMEM((8, width), f32),
            pltpu.VMEM((groups, 8, width), f32),
            pltpu.SemaphoreType.DMA((6,)),
            pltpu.SemaphoreType.DMA((7,)),
            pltpu.SemaphoreType.DMA((7,)),
            pltpu.SemaphoreType.DMA((7,)),
        ],
        compiler_params=pltpu.CompilerParams(
            collective_id=0, has_side_effects=True, vmem_limit_bytes=40 * 2**20
        ),
    )(
        held(ids),
        held(gate_logits),
        sink_logits,
        held(q.reshape(rows, width)),
        held(k.reshape(rows, width)),
        held(v.reshape(rows, width)),
        held(og),
    )


def publish_kernel(count, *refs):
    sources, targets, done = refs[:count], refs[count : 2 * count], refs[2 * count]
    copies = [
        pltpu.make_async_copy(source, target, done.at[n])
        for n, (source, target) in enumerate(zip(sources, targets))
    ]
    for copy in copies:
        copy.start()
    for copy in copies:
        copy.wait()


def publish(*arrays):
    count = len(arrays)
    places_in = [pl.BlockSpec(memory_space=pltpu.VMEM)] * (count - 1)

    def body(*refs):
        publish_kernel(count, *refs)

    return pl.pallas_call(
        body,
        out_shape=tuple(jax.ShapeDtypeStruct(a.shape, a.dtype) for a in arrays),
        in_specs=places_in + [pl.BlockSpec(memory_space=pltpu.SMEM)],
        out_specs=(pl.BlockSpec(memory_space=pltpu.HBM),) * count,
        scratch_shapes=[pltpu.SemaphoreType.DMA((count,))],
        compiler_params=pltpu.CompilerParams(vmem_limit_bytes=4 * 2**20),
    )(*arrays)


def per_device(head_ids, query_slots, key_slots, value_slots, gate_logits, sink_logits, out_grad):
    results = whole(
        lax.axis_size("dp"),
        lax.axis_size("head"),
        head_ids[0].T,
        gate_logits[0].T,
        sink_logits,
        query_slots[0],
        key_slots[0],
        value_slots[0],
        out_grad[0],
    )
    mixed, qgrad, kgrad, vgrad, gate_grad, sink_grad = publish(*results)
    return mixed[None], qgrad[None], kgrad[None], vgrad[None], gate_grad.T[None], sink_grad


def solution(mesh):
    rows3 = P("dp", "head", None)
    rows4 = P("dp", "head", None, None)
    return jax.shard_map(
        per_device,
        mesh=mesh,
        in_specs=(rows3, rows4, rows4, rows4, rows3, P("head"), rows4),
        out_specs=(rows4, rows4, rows4, rows4, rows3, P("head")),
        check_vma=False,
    )
```

```python
import math

import jax
import jax.numpy as jnp
from jax import lax
from jax.experimental import pallas as pl
from jax.experimental.pallas import tpu as pltpu
from jax.sharding import PartitionSpec as P

HEADS = 64
SLOT = 32
RING = 16
DEAD = 2.0**100
MASKED = -1e30
BLOCK = 256
MESH = pl.DeviceIdType.MESH
f32, bf16 = jnp.float32, jnp.bfloat16


def dot(a, b, dims=((1,), (0,))):
    return lax.dot_general(a, b, (dims, ((), ())), preferred_element_type=f32)


def iota(shape, dim):
    return lax.broadcasted_iota(jnp.int32, shape, dim)


def one_hot(mask):
    return jnp.where(mask, 1.0, 0.0).astype(bf16)


def block_at(n):
    return pl.ds(pl.multiple_of(n * BLOCK, BLOCK), BLOCK)


def places(ids, rows):
    slots, tokens = ids.shape
    head = iota((HEADS, tokens), 0)
    named = [head == ids[j : j + 1] for j in range(slots)]
    count = sum(jnp.where(mask, 1.0, 0.0) for mask in named).astype(bf16)
    earlier = dot(count, one_hot(iota((tokens, tokens), 0) < iota((tokens, tokens), 1)))
    rank = jnp.concatenate(
        [jnp.sum(jnp.where(mask, earlier, 0.0), axis=0, keepdims=True) for mask in named], axis=0
    )
    spread = one_hot(iota((tokens, rows), 0) == iota((tokens, rows), 1) // slots)
    place = dot(ids.astype(f32).astype(bf16), spread) * SLOT + dot(rank.astype(bf16), spread)
    mine = iota((slots, rows), 0) == iota((slots, rows), 1) % slots
    return jnp.sum(jnp.where(mine, place, 0.0), axis=0, keepdims=True).astype(jnp.int32)


def pack(place, wide, send, first, last):
    rows, width = wide.shape[0], wide.shape[1] // 4
    ones = jnp.ones((rows, width), bf16)
    size = 2 * BLOCK

    def chunk(c, carry):
        slot = c * size + iota((size, rows), 0)
        pick = one_hot(slot == place)
        moved = dot(pick, wide[:, first * width : last * width])
        for a in range(first, last):
            part = moved[:, (a - first) * width : (a - first + 1) * width]
            if a == 1:
                live = dot(pick, ones)
                part = jnp.where((live < 0.5) & (iota((size, width), 1) == 0), DEAD, part)
            send[a, pl.ds(pl.multiple_of(c * size, size), size), :] = part.astype(bf16)
        return carry

    lax.fori_loop(0, send.shape[1] // size, chunk, 0)


def forward(recv, sink, out, probs, strip, bias, sink_share, factor):
    blocks = recv.shape[1] // BLOCK
    half = recv.shape[2]
    first = one_hot(iota((8, half), 1) == 0)

    def bias_block(j, carry):
        mark = dot(first, recv[1, block_at(j), :], ((1,), (1,)))
        bias[j] = jnp.where(mark > 0.5 * DEAD, MASKED, 0.0)
        return carry

    lax.fori_loop(0, blocks, bias_block, 0)
    causal = iota((BLOCK, BLOCK), 1) <= iota((BLOCK, BLOCK), 0)

    def query_block(i, carry):
        query = recv[0, block_at(i), :]

        def scores(j):
            raw = dot(query, recv[1, block_at(j), :], ((1,), (1,))) * factor
            return jnp.where(bias[j][0:1] < 0.0, MASKED, raw)

        def halves(tile):
            return [tile[:, n * half : (n + 1) * half] for n in range(BLOCK // half)]

        def score_step(j, top):
            tile = scores(j)
            strip[j] = tile
            for part in halves(tile):
                top = jnp.maximum(top, part)
            return top

        top = lax.fori_loop(0, i, score_step, jnp.full((BLOCK, half), sink, f32))
        tile = jnp.where(causal, scores(i), MASKED)
        strip[i] = tile
        for part in halves(tile):
            top = jnp.maximum(top, part)
        top = jnp.max(top, axis=1, keepdims=True)

        def sum_step(j, total):
            weight = jnp.exp2(strip[j] - top)
            strip[j] = weight
            for part in halves(weight):
                total = total + part
            return total

        zero = jnp.zeros((BLOCK, half), f32)
        total = lax.fori_loop(0, i + 1, sum_step, zero)
        sink_part = jnp.exp2(sink - top)
        scale = 1.0 / (jnp.sum(total, axis=1, keepdims=True) + sink_part)

        def value_step(j, acc):
            weight = (strip[j] * scale).astype(bf16)
            probs[i, j] = weight
            return acc + dot(weight, recv[2, block_at(j), :])

        acc = lax.fori_loop(0, i + 1, value_step, zero)
        out[0, block_at(i), :] = acc.astype(bf16)
        sink_share[block_at(i), :] = jnp.broadcast_to(sink_part * scale, (BLOCK, half))
        return carry

    lax.fori_loop(0, blocks, query_block, 0)


def backward(recv, out, probs, sink_share, kgrad, vgrad, root):
    blocks = recv.shape[1] // BLOCK
    width = recv.shape[2]
    kgrad[...] = jnp.zeros_like(kgrad)
    vgrad[...] = jnp.zeros_like(vgrad)

    def query_block(i, sink_sum):
        at = block_at(i)
        query, cot = recv[0, at, :], recv[3, at, :]
        delta = jnp.sum(cot.astype(f32) * out[0, at, :].astype(f32), axis=1, keepdims=True)
        sink_sum = sink_sum - jnp.sum(sink_share[at, :] * delta, axis=0, keepdims=True)

        def key_step(j, qgrad):
            there = block_at(j)
            keys, values = recv[1, there, :], recv[2, there, :]
            weight = probs[i, j]
            dprob = dot(cot, values, ((1,), (1,)))
            dscore = (weight.astype(f32) * (dprob - delta)).astype(bf16)
            kgrad[there, :] += dot(dscore, query, ((0,), (0,)))
            vgrad[there, :] += dot(weight, cot, ((0,), (0,)))
            return qgrad + dot(dscore, keys)

        qgrad = lax.fori_loop(0, i + 1, key_step, jnp.zeros((BLOCK, width), f32))
        out[1, at, :] = (root * qgrad).astype(bf16)
        return sink_sum

    sink_sum = lax.fori_loop(0, blocks, query_block, jnp.zeros((1, width), f32))

    def round_block(j, carry):
        there = block_at(j)
        out[2, there, :] = (root * kgrad[there, :]).astype(bf16)
        out[3, there, :] = vgrad[there, :].astype(bf16)
        return carry

    lax.fori_loop(0, blocks, round_block, 0)
    return sink_sum


def whole_kernel(
    groups,
    devices,
    ids_hbm,
    gate_hbm,
    sink_ref,
    q_ref,
    k_ref,
    v_ref,
    og_ref,
    mixed_ref,
    qg_ref,
    kg_ref,
    vg_ref,
    gg_ref,
    sink_out,
    ids_ref,
    gate_ref,
    wide,
    og,
    gate_rows,
    gate_sums,
    place_col,
    pick,
    send,
    recv,
    ret,
    back,
    probs,
    strip,
    bias,
    sink_share,
    kgrad,
    vgrad,
    sink_mine,
    sink_all,
    load,
    near,
    sent,
    got,
):
    dp, me = lax.axis_index("dp"), lax.axis_index("head")
    rows, width = q_ref.shape
    tokens, slots, _ = og.shape

    def peers(body):
        def step(n, carry):
            body(lax.rem(me + n, devices))
            return carry

        lax.fori_loop(1, devices, step, 0)

    def group_peers(body):
        def step(n, carry):
            body(lax.rem(dp + n, groups))
            return carry

        lax.fori_loop(1, groups, step, 0)

    loads = [
        pltpu.make_async_copy(ref, wide.at[:, pl.ds(a * width, width)], load.at[a])
        for a, ref in enumerate((q_ref, k_ref, v_ref))
    ] + [
        pltpu.make_async_copy(ref, held, load.at[a])
        for a, ref, held in (
            (3, og_ref, og),
            (4, ids_hbm, ids_ref),
            (5, gate_hbm, gate_ref),
        )
    ]
    for copy in loads:
        copy.start()
    barrier = pltpu.get_barrier_semaphore()
    lines = devices // RING

    def greet(n, carry):
        d = lax.rem(n, lines) * RING + n // lines

        @pl.when(d != me)
        def _():
            pl.semaphore_signal(barrier, 1, device_id=(dp, d), device_id_type=MESH)

        return carry

    lax.fori_loop(0, devices, greet, 0)
    group_peers(lambda g: pl.semaphore_signal(barrier, 1, device_id=(g, me), device_id_type=MESH))

    for copy in loads:
        copy.wait()
    place = places(ids_ref[...], rows)
    pack(place, wide, send, 0, 3)
    pl.semaphore_wait(barrier, devices - 1 + groups - 1)

    def at(d):
        return pl.ds(pl.multiple_of(d * SLOT, SLOT), SLOT)

    stages = (
        (send, recv, pl.ds(0, 3)),
        (send, recv, pl.ds(3, 1)),
        (ret, back, pl.ds(0, 1)),
        (ret, back, pl.ds(1, 1)),
        (ret, back, pl.ds(2, 1)),
        (ret, back, pl.ds(3, 1)),
    )

    def own(phase):
        source, target, arrays = stages[phase]
        return pltpu.make_async_copy(
            source.at[arrays, at(me)], target.at[arrays, at(me)], near.at[phase]
        )

    def begin(phase):
        source, target, arrays = stages[phase]
        own(phase).start()
        peers(
            lambda d: pltpu.make_async_remote_copy(
                src_ref=source.at[arrays, at(d)],
                dst_ref=target.at[arrays, at(me)],
                send_sem=sent.at[phase],
                recv_sem=got.at[phase],
                device_id=(dp, d),
                device_id_type=MESH,
            ).start()
        )

    def all_of(ref, arrays, sem):
        piece = ref.at[arrays, pl.ds(0, (devices - 1) * SLOT)]
        pltpu.make_async_copy(piece, piece, sem).wait()

    def arrived(phase):
        _, target, arrays = stages[phase]
        own(phase).wait()
        all_of(target, arrays, got.at[phase])

    root = 1.0 / math.sqrt(width)
    begin(0)
    logits = gate_ref[...]
    shifted = jnp.exp(logits - jnp.max(logits, axis=0, keepdims=True))
    gate_rows[...] = (shifted / jnp.sum(shifted, axis=0, keepdims=True)).T
    cot = gate_rows[...][:, :, None] * og[...].astype(f32)
    wide[:, 3 * width :] = cot.astype(bf16).reshape(rows, width)

    pack(place, wide, send, 3, 4)
    begin(1)
    place_col[...] = jnp.broadcast_to(place, (8, rows)).T

    def pick_block(c, carry):
        slot = iota((BLOCK, HEADS * SLOT), 1)
        pick[block_at(c), :] = one_hot(slot == place_col[block_at(c), 0:1])
        return carry

    lax.fori_loop(0, rows // BLOCK, pick_block, 0)
    arrived(0)
    sink = sink_ref[0] * math.log2(math.e)
    forward(recv, sink, ret, probs, strip, bias, sink_share, root * math.log2(math.e))
    begin(2)
    arrived(1)
    sink_sum = backward(recv, ret, probs, sink_share, kgrad, vgrad, root)
    for phase in (3, 4, 5):
        begin(phase)
    sink_mine[...] = jnp.broadcast_to(sink_sum, sink_mine.shape)
    group_peers(
        lambda g: pltpu.make_async_remote_copy(
            src_ref=sink_mine,
            dst_ref=sink_all.at[dp],
            send_sem=sent.at[6],
            recv_sem=got.at[6],
            device_id=(g, me),
            device_id_type=MESH,
        ).start()
    )
    own_sink = pltpu.make_async_copy(sink_mine, sink_all.at[dp], near.at[6])
    own_sink.start()

    step = BLOCK // slots

    def collect(a, store):
        def chunk(c, carry):
            part = dot(pick[block_at(c), :], back[a])
            store(pl.ds(pl.multiple_of(c * step, step), step), part.reshape(step, slots, width))
            return carry

        lax.fori_loop(0, rows // BLOCK, chunk, 0)

    def store_mixed(here, part):
        mixed_ref[here] = (gate_rows[here][:, :, None] * part).astype(bf16)
        gate_sums[here] = jnp.sum(og[here].astype(f32) * part, axis=-1)

    arrived(2)
    collect(0, store_mixed)
    gate = gate_rows[...]
    gate_sum = gate_sums[...]
    mean = jnp.sum(gate * gate_sum, axis=-1, keepdims=True)
    gg_ref[...] = (gate * (gate_sum - mean)).T
    others = sink_all.at[pl.ds(0, groups - 1)]
    pltpu.make_async_copy(others, others, got.at[6]).wait()
    own_sink.wait()
    sink_out[0] = jnp.sum(jnp.sum(sink_all[...], axis=0)[0:1, 0:1])
    for a, ref in ((1, qg_ref), (2, kg_ref), (3, vg_ref)):
        arrived(a + 2)

        def store(here, part, ref=ref):
            ref[here] = part.astype(bf16)

        collect(a, store)
    for phase, (source, _, arrays) in enumerate(stages):
        all_of(source, arrays, sent.at[phase])
    pltpu.make_async_copy(others, others, sent.at[6]).wait()


def held(array):
    return pltpu.with_memory_space_constraint(array, pltpu.HBM)


def whole(groups, devices, ids, gate_logits, sink_logits, q, k, v, og):
    tokens, slots, width = og.shape
    rows = tokens * slots
    padded = HEADS * SLOT
    blocks = padded // BLOCK
    vmem = pl.BlockSpec(memory_space=pltpu.VMEM)
    smem = pl.BlockSpec(memory_space=pltpu.SMEM)
    hbm = pl.BlockSpec(memory_space=pltpu.HBM)
    grad = jax.ShapeDtypeStruct((tokens, slots, width), bf16)

    def body(*refs):
        whole_kernel(groups, devices, *refs)

    return pl.pallas_call(
        body,
        out_shape=(grad,) * 4
        + (jax.ShapeDtypeStruct((slots, tokens), f32), jax.ShapeDtypeStruct((1,), f32)),
        in_specs=[hbm, hbm, smem, hbm, hbm, hbm, hbm],
        out_specs=(vmem,) * 5 + (smem,),
        scratch_shapes=[
            pltpu.VMEM((slots, tokens), jnp.int32),
            pltpu.VMEM((slots, tokens), f32),
            pltpu.VMEM((rows, 4 * width), bf16),
            pltpu.VMEM((tokens, slots, width), bf16),
            pltpu.VMEM((tokens, slots), f32),
            pltpu.VMEM((tokens, slots), f32),
            pltpu.VMEM((rows, 8), jnp.int32),
            pltpu.VMEM((rows, padded), bf16),
            pltpu.VMEM((4, padded, width), bf16),
            pltpu.VMEM((4, padded, width), bf16),
            pltpu.VMEM((4, padded, width), bf16),
            pltpu.VMEM((4, padded, width), bf16),
            pltpu.VMEM((blocks, blocks, BLOCK, BLOCK), bf16),
            pltpu.VMEM((blocks, BLOCK, BLOCK), f32),
            pltpu.VMEM((blocks, 8, BLOCK), f32),
            pltpu.VMEM((padded, width), f32),
            pltpu.VMEM((padded, width), f32),
            pltpu.VMEM((padded, width), f32),
            pltpu.VMEM((8, width), f32),
            pltpu.VMEM((groups, 8, width), f32),
            pltpu.SemaphoreType.DMA((6,)),
            pltpu.SemaphoreType.DMA((7,)),
            pltpu.SemaphoreType.DMA((7,)),
            pltpu.SemaphoreType.DMA((7,)),
        ],
        compiler_params=pltpu.CompilerParams(
            collective_id=0, has_side_effects=True, vmem_limit_bytes=40 * 2**20
        ),
    )(
        held(ids),
        held(gate_logits),
        sink_logits,
        held(q.reshape(rows, width)),
        held(k.reshape(rows, width)),
        held(v.reshape(rows, width)),
        held(og),
    )


def publish_kernel(count, *refs):
    sources, targets, done = refs[:count], refs[count : 2 * count], refs[2 * count]
    copies = [
        pltpu.make_async_copy(source, target, done.at[n])
        for n, (source, target) in enumerate(zip(sources, targets))
    ]
    for copy in copies:
        copy.start()
    for copy in copies:
        copy.wait()


def publish(*arrays):
    count = len(arrays)
    places_in = [pl.BlockSpec(memory_space=pltpu.VMEM)] * (count - 1)

    def body(*refs):
        publish_kernel(count, *refs)

    return pl.pallas_call(
        body,
        out_shape=tuple(jax.ShapeDtypeStruct(a.shape, a.dtype) for a in arrays),
        in_specs=places_in + [pl.BlockSpec(memory_space=pltpu.SMEM)],
        out_specs=(pl.BlockSpec(memory_space=pltpu.HBM),) * count,
        scratch_shapes=[pltpu.SemaphoreType.DMA((count,))],
        compiler_params=pltpu.CompilerParams(vmem_limit_bytes=4 * 2**20),
    )(*arrays)


def per_device(head_ids, query_slots, key_slots, value_slots, gate_logits, sink_logits, out_grad):
    results = whole(
        lax.axis_size("dp"),
        lax.axis_size("head"),
        head_ids[0].T,
        gate_logits[0].T,
        sink_logits,
        query_slots[0],
        key_slots[0],
        value_slots[0],
        out_grad[0],
    )
    mixed, qgrad, kgrad, vgrad, gate_grad, sink_grad = publish(*results)
    return mixed[None], qgrad[None], kgrad[None], vgrad[None], gate_grad.T[None], sink_grad


def solution(mesh):
    rows3 = P("dp", "head", None)
    rows4 = P("dp", "head", None, None)
    return jax.shard_map(
        per_device,
        mesh=mesh,
        in_specs=(rows3, rows4, rows4, rows4, rows3, P("head"), rows4),
        out_specs=(rows4, rows4, rows4, rows4, rows3, P("head")),
        check_vma=False,
    )
```
